32 devices in a mesh: dp: 8 (over z, y), grp: 4 (over x, core).
Axes of the slice: x: 2, y: 2, z: 4, core: 2. Of those that a mesh axis runs over, the one named last changes fastest.
Arguments:
- frames: bfloat16 [96, 256, 1024], P(('dp', 'grp')), may hold values from -6 to 6
- episode_len: int32 [12], replicated, may hold values from 1 to 48, 96 in all
- norm_spatial: float32 [1024], replicated, may hold values from 0.25 to 1.75
- w_sqkv: bfloat16 [1024, 3072], replicated
- w_so: bfloat16 [1024, 1024], replicated, may hold values from -0.1875 to 0.1875
- norm_temporal: float32 [1024], replicated, may hold values from 0.25 to 1.75
- w_tqkv: bfloat16 [1024, 3072], P(('dp', 'grp'))
- w_to: bfloat16 [1024, 1024], P(('dp', 'grp')), may hold values from -0.1875 to 0.1875
Outputs:
- block_out: bfloat16 [96, 256, 1024], P(('dp', 'grp'))
The draws below stay inside these ranges and needn't reach their ends.
Inputs may be any that keep to these rules, and one draw needn't show every extreme that they name: episode_len lists consecutive episodes that together cover all 96 frames; the longest has exactly 48 frames.
All inputs are finite; a program needn't handle non-finite values.
Results may differ from the reference program's by a relative error of at most 0.029.
The reference program's roundings to bfloat16 on the way count: a program that leaves them out, or rounds other values in their place, can miss the bound.
Values may be sent and summed in bfloat16 or wider, within the bound.
A program may use at most 128 MiB of HBM per device.

```python
import math
import jax
import jax.numpy as jnp
import numpy as np
from jax import lax

D = 1024
HEADS = 16
HEAD_DIM = 64
P_SIZE = 256
FRAMES = 96
MAX_EP = 48
EPISODES = 12


def draw_w_sqkv(key, part):
    key = jax.random.fold_in(key, 11)
    values = jax.random.normal(key, (D, 3 * D), jnp.float32) * D ** (-0.5)
    return values.astype(jnp.bfloat16)


def draw_w_tqkv(key, part):
    key = jax.random.fold_in(key, 23)
    values = jax.random.normal(key, (D, 3 * D), jnp.float32) * D ** (-0.5)
    return values.astype(jnp.bfloat16)


def shard_levels(own_key, shape, shards, least, high):
    def one(dim, parts):
        steps = jax.random.uniform(jax.random.fold_in(jax.random.fold_in(own_key, 6), dim), (parts,), jnp.float32, least / len(shards), high / len(shards))
        return jnp.repeat(jnp.exp(steps), shape[dim] // parts).reshape((-1,) + (1,) * (len(shape) - dim - 1))

    factor_of = one(*shards[0])
    for cut in shards[1:]:
        factor_of = factor_of * one(*cut)
    return factor_of


def profile(count, total, reach, lean):
    loads = [(1 << 20) // math.isqrt(standing ** lean) + 1 for standing in range(2, count + 1)]
    rest, holding = total - reach - (count - 1), [1] * (count - 1)
    while rest > 0:
        free = [i for i in range(count - 1) if holding[i] < reach]
        mass, budget = sum([loads[i] for i in free]), rest
        for i in free:
            extra = min(reach - holding[i], max(1, budget * loads[i] // mass), rest)
            holding[i] = holding[i] + extra
            rest = rest - extra
    return np.array([reach] + holding)


def uneven(own_key, number_of, total, limit, skew):
    if number_of == 2:
        one = jax.random.randint(own_key, (), max(1, total - limit), min(limit, total - 1) + 1)
        return jnp.stack([one, total - one])
    sizes = jnp.asarray(profile(number_of, total, limit, skew), jnp.int32)
    pairs = (number_of - 1) // 2
    source_of, taker = sizes[1:1 + 2 * pairs:2], sizes[2:2 + 2 * pairs:2]
    slack = jnp.minimum(source_of - 1, limit - taker)
    shifted = jax.random.randint(jax.random.fold_in(own_key, 1), (pairs,), 0, 1 << 20) % (slack + 1)
    sizes = sizes.at[1:1 + 2 * pairs:2].set(source_of - shifted).at[2:2 + 2 * pairs:2].set(taker + shifted)
    return sizes[jax.random.permutation(jax.random.fold_in(own_key, 2), number_of)]


def scatter_about(stream_key, dims, spread, limit, cuts=(), kind=jnp.bfloat16):
    level = shard_levels(stream_key, dims, cuts, -0.22, 0.18) if cuts else 1.0
    drawn = jax.random.normal(stream_key, dims, jnp.float32) * spread * level
    return jnp.minimum(jnp.maximum(drawn, -limit), limit).astype(kind)


def setup_inputs(seed: int = 0) -> dict:
    arg_keys = jax.random.split(jax.random.key(seed), 9)
    frames = scatter_about(arg_keys[0], (FRAMES, P_SIZE, D), 1.0, 6.0, ((0, 32),))
    episode_len = uneven(arg_keys[1], EPISODES, FRAMES, MAX_EP, 2).astype(jnp.int32)
    norm_spatial = jnp.clip(1.0 + 0.15 * jax.random.normal(arg_keys[2], (D,), jnp.float32), 0.25, 1.75)
    w_sqkv = draw_w_sqkv(jax.random.fold_in(arg_keys[8], 71), 0)
    w_so = scatter_about(arg_keys[4], (D, D), D ** -0.5, 0.1875)
    norm_temporal = jnp.clip(1.0 + 0.15 * jax.random.normal(arg_keys[5], (D,), jnp.float32), 0.25, 1.75)
    w_tqkv = draw_w_tqkv(jax.random.fold_in(arg_keys[8], 71), 0)
    w_to = scatter_about(arg_keys[7], (D, D), D ** -0.5, 0.1875, ((0, 32),))
    return {"frames": frames, "episode_len": episode_len, "norm_spatial": norm_spatial, "w_sqkv": w_sqkv, "w_so": w_so, "norm_temporal": norm_temporal, "w_tqkv": w_tqkv, "w_to": w_to}


def normed(values, gain):
    wide = values.astype(jnp.float32)
    scale = lax.rsqrt(lax.optimization_barrier(jnp.mean(wide * wide, axis=-1, keepdims=True)) + 1e-06)
    return (wide * scale * gain).astype(jnp.bfloat16)

def softmax_rows(scores):
    top = lax.optimization_barrier(jnp.max(scores, axis=-1, keepdims=True))
    weights = jnp.exp(scores - top)
    return (weights / lax.optimization_barrier(jnp.sum(weights, axis=-1, keepdims=True))).astype(jnp.bfloat16)

def reference(frames, episode_len, norm_spatial, w_sqkv, w_so, norm_temporal, w_tqkv, w_to):
    scale = HEAD_DIM ** (-0.5)

    def spatial(frame):
        hidden = normed(frame, norm_spatial)
        qkv = jnp.dot(hidden, w_sqkv, preferred_element_type=jnp.float32).astype(jnp.bfloat16)
        qkv = qkv.reshape(P_SIZE, 3, HEADS, HEAD_DIM).astype(jnp.float32)
        scores = jnp.einsum('phd,qhd->hpq', qkv[:, 0], qkv[:, 1]) * scale
        probs = softmax_rows(scores).astype(jnp.float32)
        heads = jnp.einsum('hpq,qhd->phd', probs, qkv[:, 2]).astype(jnp.bfloat16).reshape(P_SIZE, D)
        update = jnp.dot(heads, w_so, preferred_element_type=jnp.float32)
        return (frame.astype(jnp.float32) + update).astype(jnp.bfloat16)
    mixed = lax.map(spatial, frames)
    ends = jnp.cumsum(episode_len)
    position = jnp.arange(FRAMES, dtype=jnp.int32)
    episode = lax.optimization_barrier(jnp.sum((position[:, None] >= ends[None, :]).astype(jnp.int32), axis=1))
    allowed = (position[None, :] <= position[:, None]) & (episode[None, :] == episode[:, None])

    def temporal(column):
        hidden = normed(column, norm_temporal)
        qkv = jnp.dot(hidden, w_tqkv, preferred_element_type=jnp.float32).astype(jnp.bfloat16)
        qkv = qkv.reshape(FRAMES, 3, HEADS, HEAD_DIM).astype(jnp.float32)
        scores = jnp.einsum('fhd,ghd->hfg', qkv[:, 0], qkv[:, 1]) * scale
        scores = jnp.where(allowed[None], scores, -1e+30)
        probs = softmax_rows(scores).astype(jnp.float32)
        heads = jnp.einsum('hfg,ghd->fhd', probs, qkv[:, 2]).astype(jnp.bfloat16).reshape(FRAMES, D)
        return jnp.dot(heads, w_to, preferred_element_type=jnp.float32).astype(jnp.bfloat16)
    updates = lax.map(temporal, jnp.transpose(mixed, (1, 0, 2)))
    updates = jnp.transpose(updates, (1, 0, 2))
    return (mixed.astype(jnp.float32) + updates.astype(jnp.float32)).astype(jnp.bfloat16)
```

```python
import functools

import jax
import jax.numpy as jnp
from jax import lax
from jax.experimental import pallas as pl
from jax.experimental.pallas import tpu as pltpu
from jax.sharding import PartitionSpec as P

HEADS = 16
F32 = jnp.float32
BF16 = jnp.bfloat16
NT = (((1,), (1,)), ((), ()))


def normed(values, gain):
    wide = values.astype(F32)
    scale = lax.rsqrt(jnp.mean(wide * wide, axis=-1, keepdims=True) + 1e-06)
    return (wide * scale * gain).astype(BF16)


def softmax_rows(scores):
    top = jnp.max(scores, axis=-1, keepdims=True)
    weights = jnp.exp(scores - top)
    return (weights * (1.0 / jnp.sum(weights, axis=-1, keepdims=True))).astype(BF16)


def pair_heads(q2, k2, v2, bias, low):
    rows = q2.shape[0]
    q2 = q2 * jnp.asarray(0.125, BF16)
    zero = jnp.zeros_like(q2)
    both = jnp.concatenate([jnp.where(low, q2, zero), jnp.where(low, zero, q2)], axis=0)
    scores = lax.dot_general(both, k2, NT, preferred_element_type=F32)
    if bias is not None:
        scores = jnp.where(bias, scores, -1e30)
    probs = softmax_rows(scores)
    out = jnp.dot(probs, v2, preferred_element_type=F32)
    return jnp.where(low, out[:rows], out[rows:]).astype(BF16)


def spatial_kernel(frames, gain_s, w_qkv, w_o, gain_t, mixed, hidden_t, hidden, qkv, heads):
    count, tokens, width = frames.shape
    low = lax.broadcasted_iota(jnp.int32, (tokens, 128), 1) < 64

    @pl.loop(0, count)
    def _(i):
        rows = pl.ds(pl.multiple_of(i * tokens, tokens), tokens)
        hidden[rows, :] = normed(frames[i], gain_s[...])

    @pl.loop(0, 3 * width // 256)
    def _(t):
        cols = pl.ds(pl.multiple_of(t * 256, 256), 256)
        qkv[:, cols] = jnp.dot(hidden[...], w_qkv[:, cols], preferred_element_type=F32).astype(BF16)

    @pl.loop(0, count)
    def _(i):
        rows = pl.ds(pl.multiple_of(i * tokens, tokens), tokens)

        @pl.loop(0, width // 512)
        def _(g):
            for s in range(4):
                c = pl.multiple_of(g * 512 + s * 128, 128)
                heads[:, pl.ds(c, 128)] = pair_heads(
                    qkv[rows, pl.ds(c, 128)],
                    qkv[rows, pl.ds(c + width, 128)],
                    qkv[rows, pl.ds(c + 2 * width, 128)],
                    None,
                    low,
                )

        update = jnp.dot(heads[...], w_o[...], preferred_element_type=F32)
        block = (frames[i].astype(F32) + update).astype(BF16)
        mixed[i] = block
        hidden_t[i] = normed(block, gain_t[...])


def temporal_kernel(columns, allowed, w_qkv, w_o, out, wide, hidden, qkv, heads):
    total, local_pos, width = columns.shape
    lanes = range(0, width, 128)
    for g in range(0, total, 16):
        block = columns[pl.ds(g, 16)].astype(F32).reshape(16 * local_pos, width)
        for c in lanes:
            wide[c // 128, pl.ds(g * local_pos, 16 * local_pos), :] = block[:, c : c + 128]
    for p in range(local_pos):
        for c in lanes:
            hidden[pl.ds(p * total, total), pl.ds(c, 128)] = wide[
                c // 128, pl.ds(p, total, stride=local_pos), :
            ].astype(BF16)

    @pl.loop(0, 3 * width // 256)
    def _(t):
        cols = pl.ds(pl.multiple_of(t * 256, 256), 256)
        qkv[:, cols] = jnp.dot(hidden[...], w_qkv[:, cols], preferred_element_type=F32).astype(BF16)

    mask = jnp.concatenate([allowed[...], allowed[...]], axis=0) > 0.0
    low = lax.broadcasted_iota(jnp.int32, (total, 128), 1) < 64

    @pl.loop(0, local_pos)
    def _(p):
        rows = pl.ds(pl.multiple_of(p * total, total), total)
        for c in range(0, width, 128):
            heads[rows, pl.ds(c, 128)] = pair_heads(
                qkv[rows, pl.ds(c, 128)],
                qkv[rows, pl.ds(c + width, 128)],
                qkv[rows, pl.ds(c + 2 * width, 128)],
                mask,
                low,
            )

    for t in range(0, width, 256):
        update = jnp.dot(heads[...], w_o[:, pl.ds(t, 256)], preferred_element_type=F32)
        for p in range(local_pos):
            for c in range(0, 256, 128):
                wide[(t + c) // 128, pl.ds(p, total, stride=local_pos), :] = update[
                    p * total : (p + 1) * total, c : c + 128
                ]
    for g in range(0, total, 16):
        for c in lanes:
            block = wide[c // 128, pl.ds(g * local_pos, 16 * local_pos), :]
            out[pl.ds(g, 16), :, pl.ds(c, 128)] = block.reshape(16, local_pos, 128).astype(BF16)


def allowed_frames(episode_len, total):
    ends = jnp.cumsum(episode_len)
    position = jnp.arange(total, dtype=jnp.int32)
    episode = jnp.sum((position[:, None] >= ends[None, :]).astype(jnp.int32), axis=1)
    return (position[None, :] <= position[:, None]) & (episode[None, :] == episode[:, None])


VMEM = pl.BlockSpec(memory_space=pltpu.VMEM)


def fused(frames, episode_len, norm_spatial, w_sqkv, w_so, norm_temporal, w_tqkv, w_to):
    count, tokens, width = frames.shape
    full_tqkv = lax.all_gather(w_tqkv, ("dp", "grp"), axis=0, tiled=True)
    full_to = lax.all_gather(w_to, ("dp", "grp"), axis=0, tiled=True)
    rows = count * tokens
    mixed, temporal_in = pl.pallas_call(
        spatial_kernel,
        out_shape=[jax.ShapeDtypeStruct(frames.shape, BF16)] * 2,
        in_specs=[VMEM] * 5,
        out_specs=[VMEM] * 2,
        scratch_shapes=[
            pltpu.VMEM((rows, width), BF16),
            pltpu.VMEM((rows, 3 * width), BF16),
            pltpu.VMEM((tokens, width), BF16),
        ],
        compiler_params=pltpu.CompilerParams(vmem_limit_bytes=48 << 20),
        name="spatial",
    )(frames, norm_spatial.reshape(1, width), w_sqkv, w_so, norm_temporal.reshape(1, width))
    columns = lax.all_to_all(temporal_in, ("dp", "grp"), split_axis=1, concat_axis=0, tiled=True)
    total, local_pos, _ = columns.shape
    allowed = allowed_frames(episode_len, total).astype(F32)
    rows = total * local_pos
    update = pl.pallas_call(
        temporal_kernel,
        out_shape=jax.ShapeDtypeStruct(columns.shape, BF16),
        in_specs=[VMEM] * 4,
        out_specs=VMEM,
        scratch_shapes=[
            pltpu.VMEM((width // 128, rows, 128), F32),
            pltpu.VMEM((rows, width), BF16),
            pltpu.VMEM((rows, 3 * width), BF16),
            pltpu.VMEM((rows, width), BF16),
        ],
        compiler_params=pltpu.CompilerParams(vmem_limit_bytes=48 << 20),
        name="temporal",
    )(columns, allowed, full_tqkv, full_to)
    returned = lax.all_to_all(update, ("dp", "grp"), split_axis=0, concat_axis=1, tiled=True)
    return (mixed.astype(F32) + returned.astype(F32)).astype(BF16)


def local(frames, episode_len, norm_spatial, w_sqkv, w_so, norm_temporal, w_tqkv, w_to):
    count, tokens, width = frames.shape
    head_dim = width // HEADS
    scale = head_dim ** (-0.5)
    full_tqkv, full_to = (
        lax.all_gather(w_tqkv, ("dp", "grp"), axis=0, tiled=True),
        lax.all_gather(w_to, ("dp", "grp"), axis=0, tiled=True),
    )
    hidden = normed(frames, norm_spatial).reshape(count * tokens, width)
    sqkv = jnp.dot(hidden, w_sqkv, preferred_element_type=jnp.float32).astype(jnp.bfloat16)
    sqkv = sqkv.reshape(count, tokens, 3 * width)

    def spatial_frame(block):
        queries = block[:, :width].reshape(tokens, HEADS, head_dim)
        keys_part = block[:, width : 2 * width].reshape(tokens, HEADS, head_dim)
        values_part = block[:, 2 * width :].reshape(tokens, HEADS, head_dim)
        scores = (
            jnp.einsum("phd,qhd->hpq", queries, keys_part, preferred_element_type=jnp.float32)
            * scale
        )
        probs = softmax_rows(scores)
        heads = jnp.einsum("hpq,qhd->phd", probs, values_part, preferred_element_type=jnp.float32)
        return heads.astype(jnp.bfloat16).reshape(tokens, width)

    spatial_heads = lax.map(spatial_frame, sqkv).reshape(count * tokens, width)
    update = jnp.dot(spatial_heads, w_so, preferred_element_type=jnp.float32).reshape(
        count, tokens, width
    )
    mixed = (frames.astype(jnp.float32) + update).astype(jnp.bfloat16)
    temporal_in = normed(mixed, norm_temporal)
    columns = lax.all_to_all(temporal_in, ("dp", "grp"), split_axis=1, concat_axis=0, tiled=True)
    total, local_pos, _ = columns.shape
    tqkv = jnp.dot(
        columns.reshape(total * local_pos, width), full_tqkv, preferred_element_type=jnp.float32
    )
    tqkv = tqkv.astype(jnp.bfloat16).reshape(total, local_pos, 3 * width)
    ends = jnp.cumsum(episode_len)
    position = jnp.arange(total, dtype=jnp.int32)
    episode = jnp.sum((position[:, None] >= ends[None, :]).astype(jnp.int32), axis=1)
    allowed = (position[None, :] <= position[:, None]) & (episode[None, :] == episode[:, None])
    outputs = []
    for slot_index in range(local_pos):
        block = tqkv[:, slot_index]
        queries = block[:, :width].reshape(total, HEADS, head_dim)
        keys_part = block[:, width : 2 * width].reshape(total, HEADS, head_dim)
        values_part = block[:, 2 * width :].reshape(total, HEADS, head_dim)
        scores = (
            jnp.einsum("fhd,ghd->hfg", queries, keys_part, preferred_element_type=jnp.float32)
            * scale
        )
        scores = jnp.where(allowed[None], scores, -1e30)
        probs = softmax_rows(scores)
        heads = jnp.einsum("hfg,ghd->fhd", probs, values_part, preferred_element_type=jnp.float32)
        outputs.append(heads.astype(jnp.bfloat16).reshape(total, width))
    temporal_heads = jnp.stack(outputs, axis=1).reshape(total * local_pos, width)
    temporal_update = jnp.dot(temporal_heads, full_to, preferred_element_type=jnp.float32).astype(
        jnp.bfloat16
    )
    temporal_update = temporal_update.reshape(total, local_pos, width)
    returned = lax.all_to_all(
        temporal_update, ("dp", "grp"), split_axis=0, concat_axis=1, tiled=True
    )
    return (mixed.astype(jnp.float32) + returned.astype(jnp.float32)).astype(jnp.bfloat16)


def solution(mesh):
    placed = (
        P(("dp", "grp"), None, None),
        P(),
        P(),
        P(),
        P(),
        P(),
        P(("dp", "grp"), None),
        P(("dp", "grp"), None),
    )
    devices = mesh.shape["dp"] * mesh.shape["grp"]
    body = fused if devices == 32 else local
    return jax.shard_map(
        body, mesh=mesh, in_specs=placed, out_specs=P(("dp", "grp"), None, None), check_vma=False
    )
```

```python
import functools

import jax
import jax.numpy as jnp
from jax import lax
from jax.experimental import pallas as pl
from jax.experimental.pallas import tpu as pltpu
from jax.sharding import PartitionSpec as P

HEADS = 16
F32 = jnp.float32
BF16 = jnp.bfloat16
NT = (((1,), (1,)), ((), ()))


def normed(values, gain):
    wide = values.astype(F32)
    scale = lax.rsqrt(jnp.mean(wide * wide, axis=-1, keepdims=True) + 1e-06)
    return (wide * scale * gain).astype(BF16)


def softmax_rows(scores):
    top = jnp.max(scores, axis=-1, keepdims=True)
    weights = jnp.exp(scores - top)
    return (weights * (1.0 / jnp.sum(weights, axis=-1, keepdims=True))).astype(BF16)


def pair_heads(q2, k2, v2, bias, low):
    rows = q2.shape[0]
    q2 = q2 * jnp.asarray(0.125, BF16)
    zero = jnp.zeros_like(q2)
    both = jnp.concatenate([jnp.where(low, q2, zero), jnp.where(low, zero, q2)], axis=0)
    scores = lax.dot_general(both, k2, NT, preferred_element_type=F32)
    if bias is not None:
        scores = jnp.where(bias, scores, -1e30)
    probs = softmax_rows(scores)
    out = jnp.dot(probs, v2, preferred_element_type=F32)
    return jnp.where(low, out[:rows], out[rows:]).astype(BF16)


MESH_ID = pl.DeviceIdType.MESH


def place(index, groups):
    return (index // groups, lax.rem(index, groups))


def greet_all(me, devices, groups):
    barrier = pltpu.get_barrier_semaphore()

    @pl.loop(1, devices)
    def _(k):
        peer = lax.rem(me + k, devices)
        pl.semaphore_signal(barrier, inc=1, device_id=place(peer, groups), device_id_type=MESH_ID)

    return barrier


def spatial_kernel(
    groups, frames, gain_s, w_qkv, w_o, gain_t, mixed, arrived, hidden, qkv, heads, parcels,
    send_sem, recv_sem, own_sem,
):
    count, tokens, width = frames.shape
    devices, half = parcels.shape[1], width // 2
    me = lax.axis_index("dp") * groups + lax.axis_index("grp")
    barrier = greet_all(me, devices, groups)
    low = lax.broadcasted_iota(jnp.int32, (tokens, 128), 1) < 64

    @pl.loop(0, count)
    def _(i):
        rows = pl.ds(pl.multiple_of(i * tokens, tokens), tokens)
        hidden[rows, :] = normed(frames[i], gain_s[...])

    @pl.loop(0, 3 * width // 256)
    def _(t):
        cols = pl.ds(pl.multiple_of(t * 256, 256), 256)
        qkv[:, cols] = jnp.dot(hidden[...], w_qkv[:, cols], preferred_element_type=F32).astype(BF16)

    pl.semaphore_wait(barrier, devices - 1)

    @pl.loop(0, count)
    def _(i):
        rows = pl.ds(pl.multiple_of(i * tokens, tokens), tokens)

        @pl.loop(0, width // 512)
        def _(g):
            for s in range(4):
                c = pl.multiple_of(g * 512 + s * 128, 128)
                heads[:, pl.ds(c, 128)] = pair_heads(
                    qkv[rows, pl.ds(c, 128)],
                    qkv[rows, pl.ds(c + width, 128)],
                    qkv[rows, pl.ds(c + 2 * width, 128)],
                    None,
                    low,
                )

        update = jnp.dot(heads[...], w_o[...], preferred_element_type=F32)
        block = (frames[i].astype(F32) + update).astype(BF16)
        mixed[i] = block
        token = normed(block, gain_t[...]).astype(F32)
        left = token[:, :half].reshape(devices, tokens // devices, half)
        right = token[:, half:].reshape(devices, tokens // devices, half)
        parcels[i] = jnp.concatenate([left, right], axis=1).astype(BF16)
        pltpu.make_async_copy(parcels.at[i, me], arrived.at[i, me], own_sem.at[i]).start()

        @pl.loop(1, devices)
        def _(k):
            peer = lax.rem(me + k, devices)
            pltpu.make_async_remote_copy(
                src_ref=parcels.at[i, peer],
                dst_ref=arrived.at[i, me],
                send_sem=send_sem.at[i],
                recv_sem=recv_sem.at[i],
                device_id=place(peer, groups),
                device_id_type=MESH_ID,
            ).start()

    for i in range(count):
        pltpu.make_async_copy(parcels.at[i, me], arrived.at[i, me], own_sem.at[i]).wait()
        all_of = pltpu.make_async_remote_copy(
            src_ref=parcels.at[i, pl.ds(0, devices - 1)],
            dst_ref=arrived.at[i, pl.ds(0, devices - 1)],
            send_sem=send_sem.at[i],
            recv_sem=recv_sem.at[i],
            device_id=place(lax.rem(me + 1, devices), groups),
            device_id_type=MESH_ID,
        )
        all_of.wait_send()
        all_of.wait_recv()


def temporal_kernel(
    groups, arrived, allowed, w_all, mixed, out, wide, hidden, qkv, heads, parcels, returned,
    send_sem, recv_sem, own_sem,
):
    count, devices, rows16, half = arrived.shape
    local_pos, width, total = rows16 // 2, 2 * half, count * devices
    me = lax.axis_index("dp") * groups + lax.axis_index("grp")
    barrier = greet_all(me, devices, groups)
    lanes = range(0, width, 128)

    @pl.loop(0, devices)
    def _(s):
        for i in range(count):
            block = arrived[i, s].astype(F32)
            rows = pl.ds(pl.multiple_of((s * count + i) * local_pos, local_pos), local_pos)
            for c in range(0, half, 128):
                wide[c // 128, rows, :] = block[:local_pos, c : c + 128]
                wide[(half + c) // 128, rows, :] = block[local_pos:, c : c + 128]

    for p in range(local_pos):
        for c in lanes:
            hidden[pl.ds(p * total, total), pl.ds(c, 128)] = wide[
                c // 128, pl.ds(p, total, stride=local_pos), :
            ].astype(BF16)

    @pl.loop(0, 3 * width // 256)
    def _(t):
        cols = pl.ds(pl.multiple_of(t * 256, 256), 256)
        qkv[:, cols] = jnp.dot(hidden[...], w_all[:, cols], preferred_element_type=F32).astype(BF16)

    mask = jnp.concatenate([allowed[...], allowed[...]], axis=0) > 0.0
    low = lax.broadcasted_iota(jnp.int32, (total, 128), 1) < 64

    @pl.loop(0, local_pos)
    def _(p):
        rows = pl.ds(pl.multiple_of(p * total, total), total)
        for c in range(0, width, 128):
            heads[rows, pl.ds(c, 128)] = pair_heads(
                qkv[rows, pl.ds(c, 128)],
                qkv[rows, pl.ds(c + width, 128)],
                qkv[rows, pl.ds(c + 2 * width, 128)],
                mask,
                low,
            )

    for t in range(0, width, 256):
        update = jnp.dot(heads[...], w_all[:, pl.ds(3 * width + t, 256)], preferred_element_type=F32)
        for p in range(local_pos):
            for c in range(0, 256, 128):
                wide[(t + c) // 128, pl.ds(p, total, stride=local_pos), :] = update[
                    p * total : (p + 1) * total, c : c + 128
                ]
    pl.semaphore_wait(barrier, devices - 1)

    @pl.loop(1, devices + 1)
    def _(k):
        peer = lax.rem(me + k, devices)
        for i in range(count):
            rows = pl.ds(pl.multiple_of((peer * count + i) * local_pos, local_pos), local_pos)
            for c in range(0, half, 128):
                block = jnp.concatenate(
                    [wide[c // 128, rows, :], wide[(half + c) // 128, rows, :]], axis=0
                )
                parcels[peer, pl.ds(i * rows16, rows16), pl.ds(c, 128)] = block.astype(BF16)

        @pl.when(k < devices)
        def _():
            pltpu.make_async_remote_copy(
                src_ref=parcels.at[peer],
                dst_ref=returned.at[me],
                send_sem=send_sem,
                recv_sem=recv_sem,
                device_id=place(peer, groups),
                device_id_type=MESH_ID,
            ).start()

    own = pltpu.make_async_copy(parcels.at[me], returned.at[me], own_sem)
    own.start()
    own.wait()
    all_of = pltpu.make_async_remote_copy(
        src_ref=parcels.at[pl.ds(0, devices - 1)],
        dst_ref=returned.at[pl.ds(0, devices - 1)],
        send_sem=send_sem,
        recv_sem=recv_sem,
        device_id=place(lax.rem(me + 1, devices), groups),
        device_id_type=MESH_ID,
    )
    all_of.wait_recv()

    @pl.loop(0, devices // 2)
    def _(j):
        for i in range(count):
            first = returned[2 * j, pl.ds(i * rows16, rows16), :].astype(F32)
            second = returned[2 * j + 1, pl.ds(i * rows16, rows16), :].astype(F32)
            rows = pl.ds(pl.multiple_of(j * rows16, rows16), rows16)
            for h in range(2):
                part = slice(h * local_pos, (h + 1) * local_pos)
                update = jnp.concatenate([first[part], second[part]], axis=0)
                cols = pl.ds(h * half, half)
                out[i, rows, cols] = (mixed[i, rows, cols].astype(F32) + update).astype(BF16)

    all_of.wait_send()


def allowed_frames(episode_len, total):
    ends = jnp.cumsum(episode_len)
    position = jnp.arange(total, dtype=jnp.int32)
    episode = jnp.sum((position[:, None] >= ends[None, :]).astype(jnp.int32), axis=1)
    return (position[None, :] <= position[:, None]) & (episode[None, :] == episode[:, None])


VMEM = pl.BlockSpec(memory_space=pltpu.VMEM)


def fused(groups, frames, episode_len, norm_spatial, w_sqkv, w_so, norm_temporal, w_tqkv, w_to):
    count, tokens, width = frames.shape
    devices = width // w_to.shape[0]
    w_mine = jnp.concatenate([w_tqkv, w_to], axis=1)
    w_all = lax.all_gather(w_mine, ("dp", "grp"), axis=0, tiled=True)
    rows, total, half = count * tokens, count * devices, width // 2
    block = 2 * tokens // devices
    mixed, arrived = pl.pallas_call(
        functools.partial(spatial_kernel, groups),
        out_shape=[
            jax.ShapeDtypeStruct(frames.shape, BF16),
            jax.ShapeDtypeStruct((count, devices, block, half), BF16),
        ],
        in_specs=[VMEM] * 5,
        out_specs=[VMEM, pl.BlockSpec(memory_space=pl.ANY)],
        scratch_shapes=[
            pltpu.VMEM((rows, width), BF16),
            pltpu.VMEM((rows, 3 * width), BF16),
            pltpu.VMEM((tokens, width), BF16),
            pltpu.VMEM((count, devices, block, half), BF16),
            pltpu.SemaphoreType.DMA((count,)),
            pltpu.SemaphoreType.DMA((count,)),
            pltpu.SemaphoreType.DMA((count,)),
        ],
        compiler_params=pltpu.CompilerParams(
            vmem_limit_bytes=48 << 20, collective_id=0, has_side_effects=True
        ),
        name="spatial",
    )(frames, norm_spatial.reshape(1, width), w_sqkv, w_so, norm_temporal.reshape(1, width))
    allowed = allowed_frames(episode_len, total).astype(F32)
    return pl.pallas_call(
        functools.partial(temporal_kernel, groups),
        out_shape=jax.ShapeDtypeStruct(frames.shape, BF16),
        in_specs=[VMEM] * 4,
        out_specs=VMEM,
        scratch_shapes=[
            pltpu.VMEM((width // 128, rows, 128), F32),
            pltpu.VMEM((rows, width), BF16),
            pltpu.VMEM((rows, 3 * width), BF16),
            pltpu.VMEM((rows, width), BF16),
            pltpu.VMEM((devices, count * block, half), BF16),
            pltpu.VMEM((devices, count * block, half), BF16),
            pltpu.SemaphoreType.DMA,
            pltpu.SemaphoreType.DMA,
            pltpu.SemaphoreType.DMA,
        ],
        compiler_params=pltpu.CompilerParams(
            vmem_limit_bytes=48 << 20, collective_id=1, has_side_effects=True
        ),
        name="temporal",
    )(arrived, allowed, w_all, mixed)


def local(frames, episode_len, norm_spatial, w_sqkv, w_so, norm_temporal, w_tqkv, w_to):
    count, tokens, width = frames.shape
    head_dim = width // HEADS
    scale = head_dim ** (-0.5)
    full_tqkv, full_to = (
        lax.all_gather(w_tqkv, ("dp", "grp"), axis=0, tiled=True),
        lax.all_gather(w_to, ("dp", "grp"), axis=0, tiled=True),
    )
    hidden = normed(frames, norm_spatial).reshape(count * tokens, width)
    sqkv = jnp.dot(hidden, w_sqkv, preferred_element_type=jnp.float32).astype(jnp.bfloat16)
    sqkv = sqkv.reshape(count, tokens, 3 * width)

    def spatial_frame(block):
        queries = block[:, :width].reshape(tokens, HEADS, head_dim)
        keys_part = block[:, width : 2 * width].reshape(tokens, HEADS, head_dim)
        values_part = block[:, 2 * width :].reshape(tokens, HEADS, head_dim)
        scores = (
            jnp.einsum("phd,qhd->hpq", queries, keys_part, preferred_element_type=jnp.float32)
            * scale
        )
        probs = softmax_rows(scores)
        heads = jnp.einsum("hpq,qhd->phd", probs, values_part, preferred_element_type=jnp.float32)
        return heads.astype(jnp.bfloat16).reshape(tokens, width)

    spatial_heads = lax.map(spatial_frame, sqkv).reshape(count * tokens, width)
    update = jnp.dot(spatial_heads, w_so, preferred_element_type=jnp.float32).reshape(
        count, tokens, width
    )
    mixed = (frames.astype(jnp.float32) + update).astype(jnp.bfloat16)
    temporal_in = normed(mixed, norm_temporal)
    columns = lax.all_to_all(temporal_in, ("dp", "grp"), split_axis=1, concat_axis=0, tiled=True)
    total, local_pos, _ = columns.shape
    tqkv = jnp.dot(
        columns.reshape(total * local_pos, width), full_tqkv, preferred_element_type=jnp.float32
    )
    tqkv = tqkv.astype(jnp.bfloat16).reshape(total, local_pos, 3 * width)
    ends = jnp.cumsum(episode_len)
    position = jnp.arange(total, dtype=jnp.int32)
    episode = jnp.sum((position[:, None] >= ends[None, :]).astype(jnp.int32), axis=1)
    allowed = (position[None, :] <= position[:, None]) & (episode[None, :] == episode[:, None])
    outputs = []
    for slot_index in range(local_pos):
        block = tqkv[:, slot_index]
        queries = block[:, :width].reshape(total, HEADS, head_dim)
        keys_part = block[:, width : 2 * width].reshape(total, HEADS, head_dim)
        values_part = block[:, 2 * width :].reshape(total, HEADS, head_dim)
        scores = (
            jnp.einsum("fhd,ghd->hfg", queries, keys_part, preferred_element_type=jnp.float32)
            * scale
        )
        scores = jnp.where(allowed[None], scores, -1e30)
        probs = softmax_rows(scores)
        heads = jnp.einsum("hfg,ghd->fhd", probs, values_part, preferred_element_type=jnp.float32)
        outputs.append(heads.astype(jnp.bfloat16).reshape(total, width))
    temporal_heads = jnp.stack(outputs, axis=1).reshape(total * local_pos, width)
    temporal_update = jnp.dot(temporal_heads, full_to, preferred_element_type=jnp.float32).astype(
        jnp.bfloat16
    )
    temporal_update = temporal_update.reshape(total, local_pos, width)
    returned = lax.all_to_all(
        temporal_update, ("dp", "grp"), split_axis=0, concat_axis=1, tiled=True
    )
    return (mixed.astype(jnp.float32) + returned.astype(jnp.float32)).astype(jnp.bfloat16)


def solution(mesh):
    placed = (
        P(("dp", "grp"), None, None),
        P(),
        P(),
        P(),
        P(),
        P(),
        P(("dp", "grp"), None),
        P(("dp", "grp"), None),
    )
    devices = mesh.shape["dp"] * mesh.shape["grp"]
    body = functools.partial(fused, mesh.shape["grp"]) if devices == 32 else local
    return jax.shard_map(
        body, mesh=mesh, in_specs=placed, out_specs=P(("dp", "grp"), None, None), check_vma=False
    )
```

```python
import functools

import jax
import jax.numpy as jnp
from jax import lax
from jax.experimental import pallas as pl
from jax.experimental.pallas import tpu as pltpu
from jax.sharding import PartitionSpec as P

HEADS = 16
F32 = jnp.float32
BF16 = jnp.bfloat16
NT = (((1,), (1,)), ((), ()))


def normed(values, gain):
    wide = values.astype(F32)
    scale = lax.rsqrt(jnp.mean(wide * wide, axis=-1, keepdims=True) + 1e-06)
    return (wide * scale * gain).astype(BF16)


def softmax_rows(scores):
    top = jnp.max(scores, axis=-1, keepdims=True)
    weights = jnp.exp(scores - top)
    return (weights * (1.0 / jnp.sum(weights, axis=-1, keepdims=True))).astype(BF16)


def pair_heads(q2, k2, v2, bias, low):
    rows = q2.shape[0]
    q2 = q2 * jnp.asarray(0.125, BF16)
    zero = jnp.zeros_like(q2)
    both = jnp.concatenate([jnp.where(low, q2, zero), jnp.where(low, zero, q2)], axis=0)
    scores = lax.dot_general(both, k2, NT, preferred_element_type=F32)
    if bias is not None:
        scores = jnp.where(bias, scores, -1e30)
    probs = softmax_rows(scores)
    out = jnp.dot(probs, v2, preferred_element_type=F32)
    return jnp.where(low, out[:rows], out[rows:]).astype(BF16)


MESH_ID = pl.DeviceIdType.MESH


def relay(groups, me, mine, full, send_sem, recv_sem):
    z, y, x, core = me // 8, lax.rem(me // 4, 2), lax.rem(me // 2, 2), lax.rem(me, 2)

    def index(z, y, x, core):
        return ((z * 2 + y) * 2 + x) * 2 + core

    mate, over_y, over_x = index(z, y, x, 1 - core), index(z, 1 - y, x, core), index(z, y, 1 - x, core)

    def send(source, slot, *peers):
        for peer in peers:
            pltpu.make_async_remote_copy(
                src_ref=source,
                dst_ref=full.at[slot],
                send_sem=send_sem,
                recv_sem=recv_sem.at[slot],
                device_id=place(peer, groups),
                device_id_type=MESH_ID,
            ).start()

    def wait(slot):
        pltpu.make_async_copy(full.at[slot], full.at[slot], recv_sem.at[slot]).wait()

    def forward(slot, *peers):
        wait(slot)
        send(full.at[slot], slot, *peers)

    def far(hop):
        return (z + 1 - 2 * lax.rem(z, 2), lax.rem(z + 2, 4), 3 - z)[hop]

    def first():
        line = [index(far(hop), y, x, core) for hop in range(3)]
        send(mine, me, line[0], over_y, over_x, line[1], line[2], mate)

    def along_z(hop):
        forward(index(far(hop), y, x, core), over_y, over_x, mate)

    def across():
        for other in range(4):
            peers = [over_x, mate] if other % 2 == 0 else [mate]
            forward(index(other, 1 - y, x, core), *peers)
            peers = [over_y, mate] if other % 2 == 1 else [mate]
            forward(index(other, y, 1 - x, core), *peers)

    def corner():
        for other in range(4):
            forward(index(other, 1 - y, 1 - x, core), mate)

    def finish():
        for other in range(16):
            wait(other * 2 + 1 - core)
        count = full.shape[0] - 1
        pltpu.make_async_remote_copy(
            src_ref=full.at[pl.ds(0, count)],
            dst_ref=full.at[pl.ds(0, count)],
            send_sem=send_sem,
            recv_sem=recv_sem.at[0],
            device_id=place(mate, groups),
            device_id_type=MESH_ID,
        ).wait_send()

    return first, along_z, across, corner, finish


def place(index, groups):
    return (index // groups, lax.rem(index, groups))


def greet_all(me, devices, groups):
    barrier = pltpu.get_barrier_semaphore()

    @pl.loop(1, devices)
    def _(k):
        peer = lax.rem(me + k, devices)
        pl.semaphore_signal(barrier, inc=1, device_id=place(peer, groups), device_id_type=MESH_ID)

    return barrier


def spatial_kernel(
    groups, frames, gain_s, w_qkv, w_o, gain_t, w_mine, mixed, arrived, full, hidden, qkv, heads,
    parcels, send_sem, recv_sem, own_sem, relay_send, relay_recv, relay_own,
):
    count, tokens, width = frames.shape
    devices, half = parcels.shape[1], width // 2
    me = lax.axis_index("dp") * groups + lax.axis_index("grp")
    barrier = greet_all(me, devices, groups)
    first, along_z, across, corner, finish = relay(groups, me, w_mine, full, relay_send, relay_recv)
    low = lax.broadcasted_iota(jnp.int32, (tokens, 128), 1) < 64

    @pl.loop(0, count)
    def _(i):
        rows = pl.ds(pl.multiple_of(i * tokens, tokens), tokens)
        hidden[rows, :] = normed(frames[i], gain_s[...])

    pl.semaphore_wait(barrier, devices - 1)
    first()
    own_shard = pltpu.make_async_copy(w_mine, full.at[me], relay_own)
    own_shard.start()

    @pl.loop(0, 3 * width // 256)
    def _(t):
        cols = pl.ds(pl.multiple_of(t * 256, 256), 256)
        qkv[:, cols] = jnp.dot(hidden[...], w_qkv[:, cols], preferred_element_type=F32).astype(BF16)

    along_z(0)

    @pl.loop(0, count)
    def _(i):
        rows = pl.ds(pl.multiple_of(i * tokens, tokens), tokens)

        @pl.loop(0, width // 512)
        def _(g):
            for s in range(4):
                c = pl.multiple_of(g * 512 + s * 128, 128)
                heads[:, pl.ds(c, 128)] = pair_heads(
                    qkv[rows, pl.ds(c, 128)],
                    qkv[rows, pl.ds(c + width, 128)],
                    qkv[rows, pl.ds(c + 2 * width, 128)],
                    None,
                    low,
                )

        update = jnp.dot(heads[...], w_o[...], preferred_element_type=F32)
        block = (frames[i].astype(F32) + update).astype(BF16)
        mixed[i] = block
        token = normed(block, gain_t[...]).astype(F32)
        left = token[:, :half].reshape(devices, tokens // devices, half)
        right = token[:, half:].reshape(devices, tokens // devices, half)
        parcels[i] = jnp.concatenate([left, right], axis=1).astype(BF16)
        pltpu.make_async_copy(parcels.at[i, me], arrived.at[i, me], own_sem.at[i]).start()

        @pl.loop(1, devices)
        def _(k):
            peer = lax.rem(me + k, devices)
            pltpu.make_async_remote_copy(
                src_ref=parcels.at[i, peer],
                dst_ref=arrived.at[i, me],
                send_sem=send_sem.at[i],
                recv_sem=recv_sem.at[i],
                device_id=place(peer, groups),
                device_id_type=MESH_ID,
            ).start()

        for hop in (1, 2):
            pl.when(i == hop - 1)(functools.partial(along_z, hop))

    across()
    corner()
    finish()
    own_shard.wait()
    for i in range(count):
        pltpu.make_async_copy(parcels.at[i, me], arrived.at[i, me], own_sem.at[i]).wait()
        all_of = pltpu.make_async_remote_copy(
            src_ref=parcels.at[i, pl.ds(0, devices - 1)],
            dst_ref=arrived.at[i, pl.ds(0, devices - 1)],
            send_sem=send_sem.at[i],
            recv_sem=recv_sem.at[i],
            device_id=place(lax.rem(me + 1, devices), groups),
            device_id_type=MESH_ID,
        )
        all_of.wait_send()
        all_of.wait_recv()


def temporal_kernel(
    groups, arrived, allowed, w_far, mixed, out, wide, hidden, qkv, heads, parcels, returned, w_all,
    send_sem, recv_sem, own_sem, load_sem,
):
    count, devices, rows16, half = arrived.shape
    local_pos, width, total = rows16 // 2, 2 * half, count * devices
    me = lax.axis_index("dp") * groups + lax.axis_index("grp")
    barrier = greet_all(me, devices, groups)
    load = pltpu.make_async_copy(w_far, w_all, load_sem)
    load.start()
    lanes = range(0, width, 128)

    @pl.loop(0, devices)
    def _(s):
        for i in range(count):
            block = arrived[i, s].astype(F32)
            rows = pl.ds(pl.multiple_of((s * count + i) * local_pos, local_pos), local_pos)
            for c in range(0, half, 128):
                wide[c // 128, rows, :] = block[:local_pos, c : c + 128]
                wide[(half + c) // 128, rows, :] = block[local_pos:, c : c + 128]

    for p in range(local_pos):
        for c in lanes:
            hidden[pl.ds(p * total, total), pl.ds(c, 128)] = wide[
                c // 128, pl.ds(p, total, stride=local_pos), :
            ].astype(BF16)

    load.wait()

    @pl.loop(0, 3 * width // 256)
    def _(t):
        cols = pl.ds(pl.multiple_of(t * 256, 256), 256)
        qkv[:, cols] = jnp.dot(hidden[...], w_all[:, cols], preferred_element_type=F32).astype(BF16)

    mask = jnp.concatenate([allowed[...], allowed[...]], axis=0) > 0.0
    low = lax.broadcasted_iota(jnp.int32, (total, 128), 1) < 64

    @pl.loop(0, local_pos)
    def _(p):
        rows = pl.ds(pl.multiple_of(p * total, total), total)
        for c in range(0, width, 128):
            heads[rows, pl.ds(c, 128)] = pair_heads(
                qkv[rows, pl.ds(c, 128)],
                qkv[rows, pl.ds(c + width, 128)],
                qkv[rows, pl.ds(c + 2 * width, 128)],
                mask,
                low,
            )

    for t in range(0, width, 256):
        update = jnp.dot(heads[...], w_all[:, pl.ds(3 * width + t, 256)], preferred_element_type=F32)
        for p in range(local_pos):
            for c in range(0, 256, 128):
                wide[(t + c) // 128, pl.ds(p, total, stride=local_pos), :] = update[
                    p * total : (p + 1) * total, c : c + 128
                ]
    pl.semaphore_wait(barrier, devices - 1)

    @pl.loop(1, devices + 1)
    def _(k):
        peer = lax.rem(me + k, devices)
        for i in range(count):
            rows = pl.ds(pl.multiple_of((peer * count + i) * local_pos, local_pos), local_pos)
            for c in range(0, half, 128):
                block = jnp.concatenate(
                    [wide[c // 128, rows, :], wide[(half + c) // 128, rows, :]], axis=0
                )
                parcels[peer, pl.ds(i * rows16, rows16), pl.ds(c, 128)] = block.astype(BF16)

        @pl.when(k < devices)
        def _():
            pltpu.make_async_remote_copy(
                src_ref=parcels.at[peer],
                dst_ref=returned.at[me],
                send_sem=send_sem,
                recv_sem=recv_sem,
                device_id=place(peer, groups),
                device_id_type=MESH_ID,
            ).start()

    own = pltpu.make_async_copy(parcels.at[me], returned.at[me], own_sem)
    own.start()
    own.wait()
    all_of = pltpu.make_async_remote_copy(
        src_ref=parcels.at[pl.ds(0, devices - 1)],
        dst_ref=returned.at[pl.ds(0, devices - 1)],
        send_sem=send_sem,
        recv_sem=recv_sem,
        device_id=place(lax.rem(me + 1, devices), groups),
        device_id_type=MESH_ID,
    )
    all_of.wait_recv()

    @pl.loop(0, devices // 2)
    def _(j):
        for i in range(count):
            first = returned[2 * j, pl.ds(i * rows16, rows16), :].astype(F32)
            second = returned[2 * j + 1, pl.ds(i * rows16, rows16), :].astype(F32)
            rows = pl.ds(pl.multiple_of(j * rows16, rows16), rows16)
            for h in range(2):
                part = slice(h * local_pos, (h + 1) * local_pos)
                update = jnp.concatenate([first[part], second[part]], axis=0)
                cols = pl.ds(h * half, half)
                out[i, rows, cols] = (mixed[i, rows, cols].astype(F32) + update).astype(BF16)

    all_of.wait_send()


def allowed_frames(episode_len, total):
    ends = jnp.cumsum(episode_len)
    position = jnp.arange(total, dtype=jnp.int32)
    episode = jnp.sum((position[:, None] >= ends[None, :]).astype(jnp.int32), axis=1)
    return (position[None, :] <= position[:, None]) & (episode[None, :] == episode[:, None])


VMEM = pl.BlockSpec(memory_space=pltpu.VMEM)
ANY = pl.BlockSpec(memory_space=pl.ANY)


def fused(groups, frames, episode_len, norm_spatial, w_sqkv, w_so, norm_temporal, w_tqkv, w_to):
    count, tokens, width = frames.shape
    devices = width // w_to.shape[0]
    w_mine = jnp.concatenate([w_tqkv, w_to], axis=1)
    rows, total, half = count * tokens, count * devices, width // 2
    block = 2 * tokens // devices
    mixed, arrived, full = pl.pallas_call(
        functools.partial(spatial_kernel, groups),
        out_shape=[
            jax.ShapeDtypeStruct(frames.shape, BF16),
            jax.ShapeDtypeStruct((count, devices, block, half), BF16),
            jax.ShapeDtypeStruct((devices,) + w_mine.shape, BF16),
        ],
        in_specs=[VMEM] * 5 + [ANY],
        out_specs=[VMEM, ANY, ANY],
        scratch_shapes=[
            pltpu.VMEM((rows, width), BF16),
            pltpu.VMEM((rows, 3 * width), BF16),
            pltpu.VMEM((tokens, width), BF16),
            pltpu.VMEM((count, devices, block, half), BF16),
            pltpu.SemaphoreType.DMA((count,)),
            pltpu.SemaphoreType.DMA((count,)),
            pltpu.SemaphoreType.DMA((count,)),
            pltpu.SemaphoreType.DMA,
            pltpu.SemaphoreType.DMA((devices,)),
            pltpu.SemaphoreType.DMA,
        ],
        compiler_params=pltpu.CompilerParams(
            vmem_limit_bytes=48 << 20, collective_id=0, has_side_effects=True
        ),
        name="spatial",
    )(frames, norm_spatial.reshape(1, width), w_sqkv, w_so, norm_temporal.reshape(1, width), w_mine)
    allowed = allowed_frames(episode_len, total).astype(F32)
    return pl.pallas_call(
        functools.partial(temporal_kernel, groups),
        out_shape=jax.ShapeDtypeStruct(frames.shape, BF16),
        in_specs=[VMEM, VMEM, ANY, VMEM],
        out_specs=VMEM,
        scratch_shapes=[
            pltpu.VMEM((width // 128, rows, 128), F32),
            pltpu.VMEM((rows, width), BF16),
            pltpu.VMEM((rows, 3 * width), BF16),
            pltpu.VMEM((rows, width), BF16),
            pltpu.VMEM((devices, count * block, half), BF16),
            pltpu.VMEM((devices, count * block, half), BF16),
            pltpu.VMEM((width, 4 * width), BF16),
            pltpu.SemaphoreType.DMA,
            pltpu.SemaphoreType.DMA,
            pltpu.SemaphoreType.DMA,
            pltpu.SemaphoreType.DMA,
        ],
        compiler_params=pltpu.CompilerParams(
            vmem_limit_bytes=48 << 20, collective_id=1, has_side_effects=True
        ),
        name="temporal",
    )(arrived, allowed, full.reshape(width, 4 * width), mixed)


def local(frames, episode_len, norm_spatial, w_sqkv, w_so, norm_temporal, w_tqkv, w_to):
    count, tokens, width = frames.shape
    head_dim = width // HEADS
    scale = head_dim ** (-0.5)
    full_tqkv, full_to = (
        lax.all_gather(w_tqkv, ("dp", "grp"), axis=0, tiled=True),
        lax.all_gather(w_to, ("dp", "grp"), axis=0, tiled=True),
    )
    hidden = normed(frames, norm_spatial).reshape(count * tokens, width)
    sqkv = jnp.dot(hidden, w_sqkv, preferred_element_type=jnp.float32).astype(jnp.bfloat16)
    sqkv = sqkv.reshape(count, tokens, 3 * width)

    def spatial_frame(block):
        queries = block[:, :width].reshape(tokens, HEADS, head_dim)
        keys_part = block[:, width : 2 * width].reshape(tokens, HEADS, head_dim)
        values_part = block[:, 2 * width :].reshape(tokens, HEADS, head_dim)
        scores = (
            jnp.einsum("phd,qhd->hpq", queries, keys_part, preferred_element_type=jnp.float32)
            * scale
        )
        probs = softmax_rows(scores)
        heads = jnp.einsum("hpq,qhd->phd", probs, values_part, preferred_element_type=jnp.float32)
        return heads.astype(jnp.bfloat16).reshape(tokens, width)

    spatial_heads = lax.map(spatial_frame, sqkv).reshape(count * tokens, width)
    update = jnp.dot(spatial_heads, w_so, preferred_element_type=jnp.float32).reshape(
        count, tokens, width
    )
    mixed = (frames.astype(jnp.float32) + update).astype(jnp.bfloat16)
    temporal_in = normed(mixed, norm_temporal)
    columns = lax.all_to_all(temporal_in, ("dp", "grp"), split_axis=1, concat_axis=0, tiled=True)
    total, local_pos, _ = columns.shape
    tqkv = jnp.dot(
        columns.reshape(total * local_pos, width), full_tqkv, preferred_element_type=jnp.float32
    )
    tqkv = tqkv.astype(jnp.bfloat16).reshape(total, local_pos, 3 * width)
    ends = jnp.cumsum(episode_len)
    position = jnp.arange(total, dtype=jnp.int32)
    episode = jnp.sum((position[:, None] >= ends[None, :]).astype(jnp.int32), axis=1)
    allowed = (position[None, :] <= position[:, None]) & (episode[None, :] == episode[:, None])
    outputs = []
    for slot_index in range(local_pos):
        block = tqkv[:, slot_index]
        queries = block[:, :width].reshape(total, HEADS, head_dim)
        keys_part = block[:, width : 2 * width].reshape(total, HEADS, head_dim)
        values_part = block[:, 2 * width :].reshape(total, HEADS, head_dim)
        scores = (
            jnp.einsum("fhd,ghd->hfg", queries, keys_part, preferred_element_type=jnp.float32)
            * scale
        )
        scores = jnp.where(allowed[None], scores, -1e30)
        probs = softmax_rows(scores)
        heads = jnp.einsum("hfg,ghd->fhd", probs, values_part, preferred_element_type=jnp.float32)
        outputs.append(heads.astype(jnp.bfloat16).reshape(total, width))
    temporal_heads = jnp.stack(outputs, axis=1).reshape(total * local_pos, width)
    temporal_update = jnp.dot(temporal_heads, full_to, preferred_element_type=jnp.float32).astype(
        jnp.bfloat16
    )
    temporal_update = temporal_update.reshape(total, local_pos, width)
    returned = lax.all_to_all(
        temporal_update, ("dp", "grp"), split_axis=0, concat_axis=1, tiled=True
    )
    return (mixed.astype(jnp.float32) + returned.astype(jnp.float32)).astype(jnp.bfloat16)


def solution(mesh):
    placed = (
        P(("dp", "grp"), None, None),
        P(),
        P(),
        P(),
        P(),
        P(),
        P(("dp", "grp"), None),
        P(("dp", "grp"), None),
    )
    devices = mesh.shape["dp"] * mesh.shape["grp"]
    body = functools.partial(fused, mesh.shape["grp"]) if devices == 32 else local
    return jax.shard_map(
        body, mesh=mesh, in_specs=placed, out_specs=P(("dp", "grp"), None, None), check_vma=False
    )
```

```python
import functools

import jax
import jax.numpy as jnp
from jax import lax
from jax.experimental import pallas as pl
from jax.experimental.pallas import tpu as pltpu
from jax.sharding import PartitionSpec as P

HEADS = 16
F32 = jnp.float32
BF16 = jnp.bfloat16
NT = (((1,), (1,)), ((), ()))


def normed(values, gain):
    wide = values.astype(F32)
    scale = lax.rsqrt(jnp.mean(wide * wide, axis=-1, keepdims=True) + 1e-06)
    return (wide * scale * gain).astype(BF16)


def softmax_rows(scores):
    top = jnp.max(scores, axis=-1, keepdims=True)
    weights = jnp.exp(scores - top)
    return (weights * (1.0 / jnp.sum(weights, axis=-1, keepdims=True))).astype(BF16)


def pair_heads(q2, k2, v2, bias, low):
    rows = q2.shape[0]
    q2 = q2 * jnp.asarray(0.125, BF16)
    zero = jnp.zeros_like(q2)
    both = jnp.concatenate([jnp.where(low, q2, zero), jnp.where(low, zero, q2)], axis=0)
    scores = lax.dot_general(both, k2, NT, preferred_element_type=F32)
    if bias is not None:
        scores = jnp.where(bias, scores, -1e30)
    probs = softmax_rows(scores)
    out = jnp.dot(probs, v2, preferred_element_type=F32)
    return jnp.where(low, out[:rows], out[rows:]).astype(BF16)


MESH_ID = pl.DeviceIdType.MESH


def relay(groups, me, mine, full, send_sem, recv_sem):
    z, y, x, core = me // 8, lax.rem(me // 4, 2), lax.rem(me // 2, 2), lax.rem(me, 2)

    def index(z, y, x, core):
        return ((z * 2 + y) * 2 + x) * 2 + core

    mate, over_y, over_x = index(z, y, x, 1 - core), index(z, 1 - y, x, core), index(z, y, 1 - x, core)

    def send(source, slot, *peers):
        for peer in peers:
            pltpu.make_async_remote_copy(
                src_ref=source,
                dst_ref=full.at[slot],
                send_sem=send_sem,
                recv_sem=recv_sem.at[slot],
                device_id=place(peer, groups),
                device_id_type=MESH_ID,
            ).start()

    def wait(slot):
        pltpu.make_async_copy(full.at[slot], full.at[slot], recv_sem.at[slot]).wait()

    def forward(slot, *peers):
        wait(slot)
        send(full.at[slot], slot, *peers)

    def far(hop):
        return (z + 1 - 2 * lax.rem(z, 2), lax.rem(z + 2, 4), 3 - z)[hop]

    def first():
        line = [index(far(hop), y, x, core) for hop in range(3)]
        send(mine, me, line[0], over_y, over_x, line[1], line[2], mate)

    def along_z(hop):
        forward(index(far(hop), y, x, core), over_y, over_x, mate)

    def across():
        for other in range(4):
            peers = [over_x, mate] if other % 2 == 0 else [mate]
            forward(index(other, 1 - y, x, core), *peers)
            peers = [over_y, mate] if other % 2 == 1 else [mate]
            forward(index(other, y, 1 - x, core), *peers)

    def corner():
        for other in range(4):
            forward(index(other, 1 - y, 1 - x, core), mate)

    def finish():
        for other in range(16):
            wait(other * 2 + 1 - core)
        count = full.shape[0] - 1
        pltpu.make_async_remote_copy(
            src_ref=full.at[pl.ds(0, count)],
            dst_ref=full.at[pl.ds(0, count)],
            send_sem=send_sem,
            recv_sem=recv_sem.at[0],
            device_id=place(mate, groups),
            device_id_type=MESH_ID,
        ).wait_send()

    return first, along_z, across, corner, finish


def place(index, groups):
    return (index // groups, lax.rem(index, groups))


def greet_all(me, devices, groups):
    barrier = pltpu.get_barrier_semaphore()

    @pl.loop(1, devices)
    def _(k):
        peer = lax.rem(me + k, devices)
        pl.semaphore_signal(barrier, inc=1, device_id=place(peer, groups), device_id_type=MESH_ID)

    return barrier


def spatial_kernel(
    groups, frames, gain_s, w_qkv_far, w_o_far, gain_t, w_mine, mixed, arrived, full, hidden, qkv, heads,
    parcels, w_qkv, w_o, load_sem, send_sem, recv_sem, own_sem, relay_send, relay_recv, relay_own,
):
    count, tokens, width = frames.shape
    devices, half = parcels.shape[1], width // 2
    me = lax.axis_index("dp") * groups + lax.axis_index("grp")
    barrier = greet_all(me, devices, groups)
    load_qkv = pltpu.make_async_copy(w_qkv_far, w_qkv, load_sem.at[0])
    load_o = pltpu.make_async_copy(w_o_far, w_o, load_sem.at[1])
    load_qkv.start()
    load_o.start()
    first, along_z, across, corner, finish = relay(groups, me, w_mine, full, relay_send, relay_recv)
    low = lax.broadcasted_iota(jnp.int32, (tokens, 128), 1) < 64

    @pl.loop(0, count)
    def _(i):
        rows = pl.ds(pl.multiple_of(i * tokens, tokens), tokens)
        hidden[rows, :] = normed(frames[i], gain_s[...])

    pl.semaphore_wait(barrier, devices - 1)
    first()
    own_shard = pltpu.make_async_copy(w_mine, full.at[me], relay_own)
    own_shard.start()
    load_qkv.wait()

    @pl.loop(0, 3 * width // 256)
    def _(t):
        cols = pl.ds(pl.multiple_of(t * 256, 256), 256)
        qkv[:, cols] = jnp.dot(hidden[...], w_qkv[:, cols], preferred_element_type=F32).astype(BF16)

    along_z(0)
    load_o.wait()

    @pl.loop(0, count)
    def _(i):
        rows = pl.ds(pl.multiple_of(i * tokens, tokens), tokens)

        @pl.loop(0, width // 512)
        def _(g):
            for s in range(4):
                c = pl.multiple_of(g * 512 + s * 128, 128)
                heads[:, pl.ds(c, 128)] = pair_heads(
                    qkv[rows, pl.ds(c, 128)],
                    qkv[rows, pl.ds(c + width, 128)],
                    qkv[rows, pl.ds(c + 2 * width, 128)],
                    None,
                    low,
                )

        update = jnp.dot(heads[...], w_o[...], preferred_element_type=F32)
        block = (frames[i].astype(F32) + update).astype(BF16)
        mixed[i] = block
        token = normed(block, gain_t[...]).astype(F32)
        left = token[:, :half].reshape(devices, tokens // devices, half)
        right = token[:, half:].reshape(devices, tokens // devices, half)
        parcels[i] = jnp.concatenate([left, right], axis=1).astype(BF16)
        pltpu.make_async_copy(parcels.at[i, me], arrived.at[i, me], own_sem.at[i]).start()

        @pl.loop(1, devices)
        def _(k):
            peer = lax.rem(me + k, devices)
            pltpu.make_async_remote_copy(
                src_ref=parcels.at[i, peer],
                dst_ref=arrived.at[i, me],
                send_sem=send_sem.at[i],
                recv_sem=recv_sem.at[i],
                device_id=place(peer, groups),
                device_id_type=MESH_ID,
            ).start()

        for hop in (1, 2):
            pl.when(i == hop - 1)(functools.partial(along_z, hop))

    across()
    corner()
    finish()
    own_shard.wait()
    for i in range(count):
        pltpu.make_async_copy(parcels.at[i, me], arrived.at[i, me], own_sem.at[i]).wait()
        all_of = pltpu.make_async_remote_copy(
            src_ref=parcels.at[i, pl.ds(0, devices - 1)],
            dst_ref=arrived.at[i, pl.ds(0, devices - 1)],
            send_sem=send_sem.at[i],
            recv_sem=recv_sem.at[i],
            device_id=place(lax.rem(me + 1, devices), groups),
            device_id_type=MESH_ID,
        )
        all_of.wait_send()
        all_of.wait_recv()


def temporal_kernel(
    groups, arrived, allowed, w_far, mixed, out, wide, hidden, qkv, heads, parcels, returned, w_all,
    send_sem, recv_sem, own_sem, load_sem,
):
    count, devices, rows16, half = arrived.shape
    local_pos, width, total = rows16 // 2, 2 * half, count * devices
    me = lax.axis_index("dp") * groups + lax.axis_index("grp")
    barrier = greet_all(me, devices, groups)
    load = pltpu.make_async_copy(w_far, w_all, load_sem)
    load.start()
    lanes = range(0, width, 128)

    @pl.loop(0, devices)
    def _(s):
        for i in range(count):
            block = arrived[i, s].astype(F32)
            rows = pl.ds(pl.multiple_of((slot_of(s) * count + i) * local_pos, local_pos), local_pos)
            for c in range(0, half, 128):
                wide[c // 128, rows, :] = block[:local_pos, c : c + 128]
                wide[(half + c) // 128, rows, :] = block[local_pos:, c : c + 128]

    for p in range(local_pos):
        for c in lanes:
            hidden[pl.ds(p * total, total), pl.ds(c, 128)] = wide[
                c // 128, pl.ds(p, total, stride=local_pos), :
            ].astype(BF16)

    load.wait()

    @pl.loop(0, 3 * width // 256)
    def _(t):
        cols = pl.ds(pl.multiple_of(t * 256, 256), 256)
        qkv[:, cols] = jnp.dot(hidden[...], w_all[:, cols], preferred_element_type=F32).astype(BF16)

    part = total // 2
    low = lax.broadcasted_iota(jnp.int32, (part, 128), 1) < 64
    mine = lax.rem(slot_of(me), devices // 2)
    for q in range(2):
        mask = allowed[q * part : (q + 1) * part, :]
        mask = jnp.concatenate([mask, mask], axis=0) > 0.0

        @pl.loop(0, local_pos)
        def _(p):
            rows = pl.ds(pl.multiple_of(p * total, total), total)
            asked = pl.ds(pl.multiple_of(p * total + q * part, part), part)
            for c in range(0, width, 128):
                heads[pl.ds(pl.multiple_of(p * part, part), part), pl.ds(c, 128)] = pair_heads(
                    qkv[asked, pl.ds(c, 128)],
                    qkv[rows, pl.ds(c + width, 128)],
                    qkv[rows, pl.ds(c + 2 * width, 128)],
                    mask,
                    low,
                )

        for t in range(0, width, 256):
            update = jnp.dot(
                heads[...], w_all[:, pl.ds(3 * width + t, 256)], preferred_element_type=F32
            )
            for p in range(local_pos):
                for c in range(0, 256, 128):
                    wide[
                        (t + c) // 128, pl.ds(q * part * local_pos + p, part, stride=local_pos), :
                    ] = update[p * part : (p + 1) * part, c : c + 128]
        if q == 0:
            pl.semaphore_wait(barrier, devices - 1)

        @pl.loop(0, devices // 2)
        def _(k):
            peer = device_of(lax.rem(mine + k + 1, devices // 2) + q * (devices // 2))
            for i in range(count):
                rows = pl.ds(pl.multiple_of((slot_of(peer) * count + i) * local_pos, local_pos), local_pos)
                for c in range(0, half, 128):
                    block = jnp.concatenate(
                        [wide[c // 128, rows, :], wide[(half + c) // 128, rows, :]], axis=0
                    )
                    parcels[peer, pl.ds(i * rows16, rows16), pl.ds(c, 128)] = block.astype(BF16)

            @pl.when(peer != me)
            def _():
                pltpu.make_async_remote_copy(
                    src_ref=parcels.at[peer],
                    dst_ref=returned.at[me],
                    send_sem=send_sem,
                    recv_sem=recv_sem,
                    device_id=place(peer, groups),
                    device_id_type=MESH_ID,
                ).start()

    own = pltpu.make_async_copy(parcels.at[me], returned.at[me], own_sem)
    own.start()
    own.wait()
    all_of = pltpu.make_async_remote_copy(
        src_ref=parcels.at[pl.ds(0, devices - 1)],
        dst_ref=returned.at[pl.ds(0, devices - 1)],
        send_sem=send_sem,
        recv_sem=recv_sem,
        device_id=place(lax.rem(me + 1, devices), groups),
        device_id_type=MESH_ID,
    )
    all_of.wait_recv()

    @pl.loop(0, devices // 2)
    def _(j):
        for i in range(count):
            first = returned[2 * j, pl.ds(i * rows16, rows16), :].astype(F32)
            second = returned[2 * j + 1, pl.ds(i * rows16, rows16), :].astype(F32)
            rows = pl.ds(pl.multiple_of(j * rows16, rows16), rows16)
            for h in range(2):
                part = slice(h * local_pos, (h + 1) * local_pos)
                update = jnp.concatenate([first[part], second[part]], axis=0)
                cols = pl.ds(h * half, half)
                out[i, rows, cols] = (mixed[i, rows, cols].astype(F32) + update).astype(BF16)

    all_of.wait_send()


def slot_of(device):
    return lax.rem(device // 4, 2) * 16 + device // 8 * 4 + lax.rem(device, 4)


def device_of(slot):
    return lax.rem(slot, 16) // 4 * 8 + slot // 16 * 4 + lax.rem(slot, 4)


def allowed_frames(episode_len, total, count):
    ends = jnp.cumsum(episode_len)
    row = jnp.arange(total, dtype=jnp.int32)
    position = device_of(row // count) * count + lax.rem(row, count)
    episode = jnp.sum((position[:, None] >= ends[None, :]).astype(jnp.int32), axis=1)
    return (position[None, :] <= position[:, None]) & (episode[None, :] == episode[:, None])


VMEM = pl.BlockSpec(memory_space=pltpu.VMEM)
ANY = pl.BlockSpec(memory_space=pl.ANY)


def fused(groups, frames, episode_len, norm_spatial, w_sqkv, w_so, norm_temporal, w_tqkv, w_to):
    count, tokens, width = frames.shape
    devices = width // w_to.shape[0]
    w_mine = jnp.concatenate([w_tqkv, w_to], axis=1)
    rows, total, half = count * tokens, count * devices, width // 2
    block = 2 * tokens // devices
    mixed, arrived, full = pl.pallas_call(
        functools.partial(spatial_kernel, groups),
        out_shape=[
            jax.ShapeDtypeStruct(frames.shape, BF16),
            jax.ShapeDtypeStruct((count, devices, block, half), BF16),
            jax.ShapeDtypeStruct((devices,) + w_mine.shape, BF16),
        ],
        in_specs=[VMEM, VMEM, ANY, ANY, VMEM, ANY],
        out_specs=[VMEM, ANY, ANY],
        scratch_shapes=[
            pltpu.VMEM((rows, width), BF16),
            pltpu.VMEM((rows, 3 * width), BF16),
            pltpu.VMEM((tokens, width), BF16),
            pltpu.VMEM((count, devices, block, half), BF16),
            pltpu.VMEM(w_sqkv.shape, BF16),
            pltpu.VMEM(w_so.shape, BF16),
            pltpu.SemaphoreType.DMA((2,)),
            pltpu.SemaphoreType.DMA((count,)),
            pltpu.SemaphoreType.DMA((count,)),
            pltpu.SemaphoreType.DMA((count,)),
            pltpu.SemaphoreType.DMA,
            pltpu.SemaphoreType.DMA((devices,)),
            pltpu.SemaphoreType.DMA,
        ],
        compiler_params=pltpu.CompilerParams(
            vmem_limit_bytes=48 << 20, collective_id=0, has_side_effects=True
        ),
        name="spatial",
    )(frames, norm_spatial.reshape(1, width), w_sqkv, w_so, norm_temporal.reshape(1, width), w_mine)
    allowed = allowed_frames(episode_len, total, count).astype(F32)
    return pl.pallas_call(
        functools.partial(temporal_kernel, groups),
        out_shape=jax.ShapeDtypeStruct(frames.shape, BF16),
        in_specs=[VMEM, VMEM, ANY, VMEM],
        out_specs=VMEM,
        scratch_shapes=[
            pltpu.VMEM((width // 128, rows, 128), F32),
            pltpu.VMEM((rows, width), BF16),
            pltpu.VMEM((rows, 3 * width), BF16),
            pltpu.VMEM((rows // 2, width), BF16),
            pltpu.VMEM((devices, count * block, half), BF16),
            pltpu.VMEM((devices, count * block, half), BF16),
            pltpu.VMEM((width, 4 * width), BF16),
            pltpu.SemaphoreType.DMA,
            pltpu.SemaphoreType.DMA,
            pltpu.SemaphoreType.DMA,
            pltpu.SemaphoreType.DMA,
        ],
        compiler_params=pltpu.CompilerParams(
            vmem_limit_bytes=48 << 20, collective_id=1, has_side_effects=True
        ),
        name="temporal",
    )(arrived, allowed, full.reshape(width, 4 * width), mixed)


def local(frames, episode_len, norm_spatial, w_sqkv, w_so, norm_temporal, w_tqkv, w_to):
    count, tokens, width = frames.shape
    head_dim = width // HEADS
    scale = head_dim ** (-0.5)
    full_tqkv, full_to = (
        lax.all_gather(w_tqkv, ("dp", "grp"), axis=0, tiled=True),
        lax.all_gather(w_to, ("dp", "grp"), axis=0, tiled=True),
    )
    hidden = normed(frames, norm_spatial).reshape(count * tokens, width)
    sqkv = jnp.dot(hidden, w_sqkv, preferred_element_type=jnp.float32).astype(jnp.bfloat16)
    sqkv = sqkv.reshape(count, tokens, 3 * width)

    def spatial_frame(block):
        queries = block[:, :width].reshape(tokens, HEADS, head_dim)
        keys_part = block[:, width : 2 * width].reshape(tokens, HEADS, head_dim)
        values_part = block[:, 2 * width :].reshape(tokens, HEADS, head_dim)
        scores = (
            jnp.einsum("phd,qhd->hpq", queries, keys_part, preferred_element_type=jnp.float32)
            * scale
        )
        probs = softmax_rows(scores)
        heads = jnp.einsum("hpq,qhd->phd", probs, values_part, preferred_element_type=jnp.float32)
        return heads.astype(jnp.bfloat16).reshape(tokens, width)

    spatial_heads = lax.map(spatial_frame, sqkv).reshape(count * tokens, width)
    update = jnp.dot(spatial_heads, w_so, preferred_element_type=jnp.float32).reshape(
        count, tokens, width
    )
    mixed = (frames.astype(jnp.float32) + update).astype(jnp.bfloat16)
    temporal_in = normed(mixed, norm_temporal)
    columns = lax.all_to_all(temporal_in, ("dp", "grp"), split_axis=1, concat_axis=0, tiled=True)
    total, local_pos, _ = columns.shape
    tqkv = jnp.dot(
        columns.reshape(total * local_pos, width), full_tqkv, preferred_element_type=jnp.float32
    )
    tqkv = tqkv.astype(jnp.bfloat16).reshape(total, local_pos, 3 * width)
    ends = jnp.cumsum(episode_len)
    position = jnp.arange(total, dtype=jnp.int32)
    episode = jnp.sum((position[:, None] >= ends[None, :]).astype(jnp.int32), axis=1)
    allowed = (position[None, :] <= position[:, None]) & (episode[None, :] == episode[:, None])
    outputs = []
    for slot_index in range(local_pos):
        block = tqkv[:, slot_index]
        queries = block[:, :width].reshape(total, HEADS, head_dim)
        keys_part = block[:, width : 2 * width].reshape(total, HEADS, head_dim)
        values_part = block[:, 2 * width :].reshape(total, HEADS, head_dim)
        scores = (
            jnp.einsum("fhd,ghd->hfg", queries, keys_part, preferred_element_type=jnp.float32)
            * scale
        )
        scores = jnp.where(allowed[None], scores, -1e30)
        probs = softmax_rows(scores)
        heads = jnp.einsum("hfg,ghd->fhd", probs, values_part, preferred_element_type=jnp.float32)
        outputs.append(heads.astype(jnp.bfloat16).reshape(total, width))
    temporal_heads = jnp.stack(outputs, axis=1).reshape(total * local_pos, width)
    temporal_update = jnp.dot(temporal_heads, full_to, preferred_element_type=jnp.float32).astype(
        jnp.bfloat16
    )
    temporal_update = temporal_update.reshape(total, local_pos, width)
    returned = lax.all_to_all(
        temporal_update, ("dp", "grp"), split_axis=0, concat_axis=1, tiled=True
    )
    return (mixed.astype(jnp.float32) + returned.astype(jnp.float32)).astype(jnp.bfloat16)


def solution(mesh):
    placed = (
        P(("dp", "grp"), None, None),
        P(),
        P(),
        P(),
        P(),
        P(),
        P(("dp", "grp"), None),
        P(("dp", "grp"), None),
    )
    devices = mesh.shape["dp"] * mesh.shape["grp"]
    body = functools.partial(fused, mesh.shape["grp"]) if devices == 32 else local
    return jax.shard_map(
        body, mesh=mesh, in_specs=placed, out_specs=P(("dp", "grp"), None, None), check_vma=False
    )
```

```python
import functools

import jax
import jax.numpy as jnp
from jax import lax
from jax.experimental import pallas as pl
from jax.experimental.pallas import tpu as pltpu
from jax.sharding import PartitionSpec as P

HEADS = 16
F32 = jnp.float32
BF16 = jnp.bfloat16
NT = (((1,), (1,)), ((), ()))


def normed(values, gain):
    wide = values.astype(F32)
    scale = lax.rsqrt(jnp.mean(wide * wide, axis=-1, keepdims=True) + 1e-06)
    return (wide * scale * gain).astype(BF16)


def softmax_rows(scores):
    top = jnp.max(scores, axis=-1, keepdims=True)
    weights = jnp.exp(scores - top)
    return (weights * (1.0 / jnp.sum(weights, axis=-1, keepdims=True))).astype(BF16)


def pair_heads(q2, k2, v2, bias, low):
    rows = q2.shape[0]
    q2 = q2 * jnp.asarray(0.125, BF16)
    zero = jnp.zeros_like(q2)
    both = jnp.concatenate([jnp.where(low, q2, zero), jnp.where(low, zero, q2)], axis=0)
    scores = lax.dot_general(both, k2, NT, preferred_element_type=F32)
    if bias is not None:
        scores = jnp.where(bias, scores, -1e30)
    probs = softmax_rows(scores)
    out = jnp.dot(probs, v2, preferred_element_type=F32)
    return jnp.where(low, out[:rows], out[rows:]).astype(BF16)


MESH_ID = pl.DeviceIdType.MESH


def relay(groups, me, mine, full, send_sem, recv_sem):
    z, y, x, core = me // 8, lax.rem(me // 4, 2), lax.rem(me // 2, 2), lax.rem(me, 2)

    def index(z, y, x, core):
        return ((z * 2 + y) * 2 + x) * 2 + core

    mate, over_y, over_x = index(z, y, x, 1 - core), index(z, 1 - y, x, core), index(z, y, 1 - x, core)

    def send(source, slot, *peers):
        for peer in peers:
            pltpu.make_async_remote_copy(
                src_ref=source,
                dst_ref=full.at[slot],
                send_sem=send_sem,
                recv_sem=recv_sem.at[slot],
                device_id=place(peer, groups),
                device_id_type=MESH_ID,
            ).start()

    def wait(slot):
        pltpu.make_async_copy(full.at[slot], full.at[slot], recv_sem.at[slot]).wait()

    def forward(slot, *peers):
        wait(slot)
        send(full.at[slot], slot, *peers)

    def far(hop):
        return (z + 1 - 2 * lax.rem(z, 2), lax.rem(z + 2, 4), 3 - z)[hop]

    def first():
        line = [index(far(hop), y, x, core) for hop in range(3)]
        send(mine, me, line[0], over_y, over_x, line[1], line[2], mate)

    def along_z(hop):
        forward(index(far(hop), y, x, core), over_y, over_x, mate)

    def across():
        for other in range(4):
            peers = [over_x, mate] if other % 2 == 0 else [mate]
            forward(index(other, 1 - y, x, core), *peers)
            peers = [over_y, mate] if other % 2 == 1 else [mate]
            forward(index(other, y, 1 - x, core), *peers)

    def corner():
        for other in range(4):
            forward(index(other, 1 - y, 1 - x, core), mate)

    def finish():
        for other in range(16):
            wait(other * 2 + 1 - core)
        count = full.shape[0] - 1
        pltpu.make_async_remote_copy(
            src_ref=full.at[pl.ds(0, count)],
            dst_ref=full.at[pl.ds(0, count)],
            send_sem=send_sem,
            recv_sem=recv_sem.at[0],
            device_id=place(mate, groups),
            device_id_type=MESH_ID,
        ).wait_send()

    return first, along_z, across, corner, finish


def place(index, groups):
    return (index // groups, lax.rem(index, groups))


def greet_all(me, devices, groups):
    barrier = pltpu.get_barrier_semaphore()

    @pl.loop(1, devices)
    def _(k):
        peer = lax.rem(me + k, devices)
        pl.semaphore_signal(barrier, inc=1, device_id=place(peer, groups), device_id_type=MESH_ID)

    return barrier


def spatial_kernel(
    groups, frames, gain_s, w_qkv_far, w_o_far, gain_t, w_mine, mixed, arrived, full, hidden, qkv, heads,
    parcels, w_qkv, w_o, load_sem, send_sem, recv_sem, own_sem, relay_send, relay_recv, relay_own,
):
    count, tokens, width = frames.shape
    devices, half = parcels.shape[1], width // 2
    me = lax.axis_index("dp") * groups + lax.axis_index("grp")
    barrier = greet_all(me, devices, groups)
    load_qkv = pltpu.make_async_copy(w_qkv_far, w_qkv, load_sem.at[0])
    load_o = pltpu.make_async_copy(w_o_far, w_o, load_sem.at[1])
    load_qkv.start()
    load_o.start()
    first, along_z, across, corner, finish = relay(groups, me, w_mine, full, relay_send, relay_recv)
    low = lax.broadcasted_iota(jnp.int32, (tokens, 128), 1) < 64

    @pl.loop(0, count)
    def _(i):
        rows = pl.ds(pl.multiple_of(i * tokens, tokens), tokens)
        hidden[rows, :] = normed(frames[i], gain_s[...])

    pl.semaphore_wait(barrier, devices - 1)
    first()
    own_shard = pltpu.make_async_copy(w_mine, full.at[me], relay_own)
    own_shard.start()
    load_qkv.wait()

    @pl.loop(0, 3 * width // 256)
    def _(t):
        cols = pl.ds(pl.multiple_of(t * 256, 256), 256)
        qkv[:, cols] = jnp.dot(hidden[...], w_qkv[:, cols], preferred_element_type=F32).astype(BF16)

    along_z(0)
    load_o.wait()

    @pl.loop(0, count)
    def _(i):
        rows = pl.ds(pl.multiple_of(i * tokens, tokens), tokens)

        @pl.loop(0, width // 512)
        def _(g):
            for s in range(4):
                c = pl.multiple_of(g * 512 + s * 128, 128)
                heads[:, pl.ds(c, 128)] = pair_heads(
                    qkv[rows, pl.ds(c, 128)],
                    qkv[rows, pl.ds(c + width, 128)],
                    qkv[rows, pl.ds(c + 2 * width, 128)],
                    None,
                    low,
                )

        update = jnp.dot(heads[...], w_o[...], preferred_element_type=F32)
        block = (frames[i].astype(F32) + update).astype(BF16)
        mixed[i] = block
        token = normed(block, gain_t[...]).astype(F32)
        left = token[:, :half].reshape(devices, tokens // devices, half)
        right = token[:, half:].reshape(devices, tokens // devices, half)
        parcels[i] = jnp.concatenate([left, right], axis=1).astype(BF16)
        pltpu.make_async_copy(parcels.at[i, me], arrived.at[i, me], own_sem.at[i]).start()

        @pl.loop(1, devices)
        def _(k):
            peer = lax.rem(me + k, devices)
            pltpu.make_async_remote_copy(
                src_ref=parcels.at[i, peer],
                dst_ref=arrived.at[i, me],
                send_sem=send_sem.at[i],
                recv_sem=recv_sem.at[i],
                device_id=place(peer, groups),
                device_id_type=MESH_ID,
            ).start()

        for hop in (1, 2):
            pl.when(i == hop - 1)(functools.partial(along_z, hop))

    across()
    corner()
    finish()
    own_shard.wait()
    for i in range(count):
        pltpu.make_async_copy(parcels.at[i, me], arrived.at[i, me], own_sem.at[i]).wait()
        all_of = pltpu.make_async_remote_copy(
            src_ref=parcels.at[i, pl.ds(0, devices - 1)],
            dst_ref=arrived.at[i, pl.ds(0, devices - 1)],
            send_sem=send_sem.at[i],
            recv_sem=recv_sem.at[i],
            device_id=place(lax.rem(me + 1, devices), groups),
            device_id_type=MESH_ID,
        )
        all_of.wait_send()
        all_of.wait_recv()


def temporal_kernel(
    groups, arrived, allowed, w_far, mixed, out, wide, hidden, qkv, heads, parcels, returned, w_all,
    send_sem, recv_sem, own_sem, load_sem,
):
    count, devices, rows16, half = arrived.shape
    local_pos, width, total = rows16 // 2, 2 * half, count * devices
    me = lax.axis_index("dp") * groups + lax.axis_index("grp")
    barrier = greet_all(me, devices, groups)
    load = pltpu.make_async_copy(w_far, w_all, load_sem)
    load.start()
    lanes = range(0, width, 128)

    @pl.loop(0, devices)
    def _(s):
        for i in range(count):
            block = arrived[i, s].astype(F32)
            rows = pl.ds(pl.multiple_of((slot_of(s) * count + i) * local_pos, local_pos), local_pos)
            for c in range(0, half, 128):
                wide[c // 128, rows, :] = block[:local_pos, c : c + 128]
                wide[(half + c) // 128, rows, :] = block[local_pos:, c : c + 128]

    for p in range(local_pos):
        for c in lanes:
            hidden[pl.ds(p * total, total), pl.ds(c, 128)] = wide[
                c // 128, pl.ds(p, total, stride=local_pos), :
            ].astype(BF16)

    load.wait()

    @pl.loop(0, 3 * width // 256)
    def _(t):
        cols = pl.ds(pl.multiple_of(t * 256, 256), 256)
        qkv[:, cols] = jnp.dot(hidden[...], w_all[:, cols], preferred_element_type=F32).astype(BF16)

    part = total // 2
    low = lax.broadcasted_iota(jnp.int32, (part, 128), 1) < 64
    mine = lax.rem(slot_of(me), devices // 2)
    for q in range(2):
        mask = allowed[q * part : (q + 1) * part, :]
        mask = jnp.concatenate([mask, mask], axis=0) > 0.0

        @pl.loop(0, local_pos)
        def _(p):
            rows = pl.ds(pl.multiple_of(p * total, total), total)
            asked = pl.ds(pl.multiple_of(p * total + q * part, part), part)
            for c in range(0, width, 128):
                heads[pl.ds(pl.multiple_of(p * part, part), part), pl.ds(c, 128)] = pair_heads(
                    qkv[asked, pl.ds(c, 128)],
                    qkv[rows, pl.ds(c + width, 128)],
                    qkv[rows, pl.ds(c + 2 * width, 128)],
                    mask,
                    low,
                )

        for t in range(0, width, 256):
            update = jnp.dot(
                heads[...], w_all[:, pl.ds(3 * width + t, 256)], preferred_element_type=F32
            )
            for p in range(local_pos):
                for c in range(0, 256, 128):
                    wide[
                        (t + c) // 128, pl.ds(q * part * local_pos + p, part, stride=local_pos), :
                    ] = update[p * part : (p + 1) * part, c : c + 128]
        if q == 0:
            pl.semaphore_wait(barrier, devices - 1)

        @pl.loop(0, devices // 2)
        def _(k):
            peer = device_of(lax.rem(mine + k + 1, devices // 2) + q * (devices // 2))
            for i in range(count):
                rows = pl.ds(pl.multiple_of((slot_of(peer) * count + i) * local_pos, local_pos), local_pos)
                for c in range(0, half, 128):
                    block = jnp.concatenate(
                        [wide[c // 128, rows, :], wide[(half + c) // 128, rows, :]], axis=0
                    )
                    parcels[peer, pl.ds(i * rows16, rows16), pl.ds(c, 128)] = block.astype(BF16)

            @pl.when(peer != me)
            def _():
                pltpu.make_async_remote_copy(
                    src_ref=parcels.at[peer],
                    dst_ref=returned.at[me],
                    send_sem=send_sem,
                    recv_sem=recv_sem,
                    device_id=place(peer, groups),
                    device_id_type=MESH_ID,
                ).start()

    own = pltpu.make_async_copy(parcels.at[me], returned.at[me], own_sem)
    own.start()
    own.wait()
    all_of = pltpu.make_async_remote_copy(
        src_ref=parcels.at[pl.ds(0, devices - 1)],
        dst_ref=returned.at[pl.ds(0, devices - 1)],
        send_sem=send_sem,
        recv_sem=recv_sem,
        device_id=place(lax.rem(me + 1, devices), groups),
        device_id_type=MESH_ID,
    )
    all_of.wait_recv()

    @pl.loop(0, devices // 2)
    def _(j):
        for i in range(count):
            first = returned[2 * j, pl.ds(i * rows16, rows16), :].astype(F32)
            second = returned[2 * j + 1, pl.ds(i * rows16, rows16), :].astype(F32)
            rows = pl.ds(pl.multiple_of(j * rows16, rows16), rows16)
            for h in range(2):
                part = slice(h * local_pos, (h + 1) * local_pos)
                update = jnp.concatenate([first[part], second[part]], axis=0)
                cols = pl.ds(h * half, half)
                out[i, rows, cols] = (mixed[i, rows, cols].astype(F32) + update).astype(BF16)

    all_of.wait_send()


def slot_of(device):
    return lax.rem(device, 2) * 16 + device // 2


def device_of(slot):
    return lax.rem(slot, 16) * 2 + slot // 16


def allowed_frames(episode_len, total, count):
    ends = jnp.cumsum(episode_len)
    row = jnp.arange(total, dtype=jnp.int32)
    position = device_of(row // count) * count + lax.rem(row, count)
    episode = jnp.sum((position[:, None] >= ends[None, :]).astype(jnp.int32), axis=1)
    return (position[None, :] <= position[:, None]) & (episode[None, :] == episode[:, None])


VMEM = pl.BlockSpec(memory_space=pltpu.VMEM)
ANY = pl.BlockSpec(memory_space=pl.ANY)


def fused(groups, frames, episode_len, norm_spatial, w_sqkv, w_so, norm_temporal, w_tqkv, w_to):
    count, tokens, width = frames.shape
    devices = width // w_to.shape[0]
    w_mine = jnp.concatenate([w_tqkv, w_to], axis=1)
    rows, total, half = count * tokens, count * devices, width // 2
    block = 2 * tokens // devices
    mixed, arrived, full = pl.pallas_call(
        functools.partial(spatial_kernel, groups),
        out_shape=[
            jax.ShapeDtypeStruct(frames.shape, BF16),
            jax.ShapeDtypeStruct((count, devices, block, half), BF16),
            jax.ShapeDtypeStruct((devices,) + w_mine.shape, BF16),
        ],
        in_specs=[VMEM, VMEM, ANY, ANY, VMEM, ANY],
        out_specs=[VMEM, ANY, ANY],
        scratch_shapes=[
            pltpu.VMEM((rows, width), BF16),
            pltpu.VMEM((rows, 3 * width), BF16),
            pltpu.VMEM((tokens, width), BF16),
            pltpu.VMEM((count, devices, block, half), BF16),
            pltpu.VMEM(w_sqkv.shape, BF16),
            pltpu.VMEM(w_so.shape, BF16),
            pltpu.SemaphoreType.DMA((2,)),
            pltpu.SemaphoreType.DMA((count,)),
            pltpu.SemaphoreType.DMA((count,)),
            pltpu.SemaphoreType.DMA((count,)),
            pltpu.SemaphoreType.DMA,
            pltpu.SemaphoreType.DMA((devices,)),
            pltpu.SemaphoreType.DMA,
        ],
        compiler_params=pltpu.CompilerParams(
            vmem_limit_bytes=48 << 20, collective_id=0, has_side_effects=True
        ),
        name="spatial",
    )(frames, norm_spatial.reshape(1, width), w_sqkv, w_so, norm_temporal.reshape(1, width), w_mine)
    allowed = allowed_frames(episode_len, total, count).astype(F32)
    return pl.pallas_call(
        functools.partial(temporal_kernel, groups),
        out_shape=jax.ShapeDtypeStruct(frames.shape, BF16),
        in_specs=[VMEM, VMEM, ANY, VMEM],
        out_specs=VMEM,
        scratch_shapes=[
            pltpu.VMEM((width // 128, rows, 128), F32),
            pltpu.VMEM((rows, width), BF16),
            pltpu.VMEM((rows, 3 * width), BF16),
            pltpu.VMEM((rows // 2, width), BF16),
            pltpu.VMEM((devices, count * block, half), BF16),
            pltpu.VMEM((devices, count * block, half), BF16),
            pltpu.VMEM((width, 4 * width), BF16),
            pltpu.SemaphoreType.DMA,
            pltpu.SemaphoreType.DMA,
            pltpu.SemaphoreType.DMA,
            pltpu.SemaphoreType.DMA,
        ],
        compiler_params=pltpu.CompilerParams(
            vmem_limit_bytes=48 << 20, collective_id=1, has_side_effects=True
        ),
        name="temporal",
    )(arrived, allowed, full.reshape(width, 4 * width), mixed)


def local(frames, episode_len, norm_spatial, w_sqkv, w_so, norm_temporal, w_tqkv, w_to):
    count, tokens, width = frames.shape
    head_dim = width // HEADS
    scale = head_dim ** (-0.5)
    full_tqkv, full_to = (
        lax.all_gather(w_tqkv, ("dp", "grp"), axis=0, tiled=True),
        lax.all_gather(w_to, ("dp", "grp"), axis=0, tiled=True),
    )
    hidden = normed(frames, norm_spatial).reshape(count * tokens, width)
    sqkv = jnp.dot(hidden, w_sqkv, preferred_element_type=jnp.float32).astype(jnp.bfloat16)
    sqkv = sqkv.reshape(count, tokens, 3 * width)

    def spatial_frame(block):
        queries = block[:, :width].reshape(tokens, HEADS, head_dim)
        keys_part = block[:, width : 2 * width].reshape(tokens, HEADS, head_dim)
        values_part = block[:, 2 * width :].reshape(tokens, HEADS, head_dim)
        scores = (
            jnp.einsum("phd,qhd->hpq", queries, keys_part, preferred_element_type=jnp.float32)
            * scale
        )
        probs = softmax_rows(scores)
        heads = jnp.einsum("hpq,qhd->phd", probs, values_part, preferred_element_type=jnp.float32)
        return heads.astype(jnp.bfloat16).reshape(tokens, width)

    spatial_heads = lax.map(spatial_frame, sqkv).reshape(count * tokens, width)
    update = jnp.dot(spatial_heads, w_so, preferred_element_type=jnp.float32).reshape(
        count, tokens, width
    )
    mixed = (frames.astype(jnp.float32) + update).astype(jnp.bfloat16)
    temporal_in = normed(mixed, norm_temporal)
    columns = lax.all_to_all(temporal_in, ("dp", "grp"), split_axis=1, concat_axis=0, tiled=True)
    total, local_pos, _ = columns.shape
    tqkv = jnp.dot(
        columns.reshape(total * local_pos, width), full_tqkv, preferred_element_type=jnp.float32
    )
    tqkv = tqkv.astype(jnp.bfloat16).reshape(total, local_pos, 3 * width)
    ends = jnp.cumsum(episode_len)
    position = jnp.arange(total, dtype=jnp.int32)
    episode = jnp.sum((position[:, None] >= ends[None, :]).astype(jnp.int32), axis=1)
    allowed = (position[None, :] <= position[:, None]) & (episode[None, :] == episode[:, None])
    outputs = []
    for slot_index in range(local_pos):
        block = tqkv[:, slot_index]
        queries = block[:, :width].reshape(total, HEADS, head_dim)
        keys_part = block[:, width : 2 * width].reshape(total, HEADS, head_dim)
        values_part = block[:, 2 * width :].reshape(total, HEADS, head_dim)
        scores = (
            jnp.einsum("fhd,ghd->hfg", queries, keys_part, preferred_element_type=jnp.float32)
            * scale
        )
        scores = jnp.where(allowed[None], scores, -1e30)
        probs = softmax_rows(scores)
        heads = jnp.einsum("hfg,ghd->fhd", probs, values_part, preferred_element_type=jnp.float32)
        outputs.append(heads.astype(jnp.bfloat16).reshape(total, width))
    temporal_heads = jnp.stack(outputs, axis=1).reshape(total * local_pos, width)
    temporal_update = jnp.dot(temporal_heads, full_to, preferred_element_type=jnp.float32).astype(
        jnp.bfloat16
    )
    temporal_update = temporal_update.reshape(total, local_pos, width)
    returned = lax.all_to_all(
        temporal_update, ("dp", "grp"), split_axis=0, concat_axis=1, tiled=True
    )
    return (mixed.astype(jnp.float32) + returned.astype(jnp.float32)).astype(jnp.bfloat16)


def solution(mesh):
    placed = (
        P(("dp", "grp"), None, None),
        P(),
        P(),
        P(),
        P(),
        P(),
        P(("dp", "grp"), None),
        P(("dp", "grp"), None),
    )
    devices = mesh.shape["dp"] * mesh.shape["grp"]
    body = functools.partial(fused, mesh.shape["grp"]) if devices == 32 else local
    return jax.shard_map(
        body, mesh=mesh, in_specs=placed, out_specs=P(("dp", "grp"), None, None), check_vma=False
    )
```
